32 devices in a mesh: row: 8 (over y, x, core), col: 4 (over z).
Axes of the slice: x: 2, y: 2, z: 4, core: 2. Of those that a mesh axis runs over, the one named last changes fastest.
Arguments:
- emissions: float32 [2, 4, 1024, 512], P(None, None, 'row', 'col'), may hold values from 0 to 101
- winds: float32 [2, 2, 1024, 512], P(None, None, 'row', 'col'), may hold values from -0.4 to 0.4
- kernels: float32 [4, 65, 65], replicated, may hold values from 0 to 4
- box_states: float32 [4, 4, 1024, 512], P(None, None, 'row', 'col'), may hold values from 0.02 to 0.3
- decay: float32 [4, 4], replicated, may hold values from 0.3 to 0.95
- fraction: float32 [4, 4], replicated, may hold values from 0.1 to 0.6
Outputs:
- new_states: float32 [4, 4, 1024, 512], P(None, None, 'row', 'col')
- surface: float32 [4, 1024, 512], P(None, 'row', 'col')
The draws below stay inside these ranges and needn't reach their ends.
All inputs are finite; a program needn't handle non-finite values.
Results may differ from the reference program's by a relative error of at most 0.0001.
Values sent between devices are 32-bit elements; how exact they have to be, the bound alone decides.
A program may use at most 64 MiB of HBM per device.

```python
import math
import jax
import jax.numpy as jnp

SPECIES = 4
BOXES = 4
KW = 65
STEPS = 2
HALF = 32
NR = 1024
NC = 512


def draw_emissions(key, part):
    k_back, k_live, k_size, k_city = jax.random.split(key, 4)
    shape = (STEPS, SPECIES, NR, NC)
    city = jnp.exp(jax.random.uniform(k_city, (NR // 8, NC // 8), jnp.float32, math.log(0.25), math.log(4.0)))
    city = jnp.repeat(jnp.repeat(city, 8, axis=0), 8, axis=1)
    live = jax.random.uniform(k_live, shape, jnp.float32) < 0.02 * city[None, None]
    amount = jnp.exp(jax.random.uniform(k_size, shape, jnp.float32, math.log(2.0), math.log(100.0)))
    back = jnp.exp(jax.random.uniform(k_back, shape, jnp.float32, math.log(0.005), math.log(0.05)))
    return (jnp.where(live, amount, 0.0) + back).astype(jnp.float32)


def draw_kernels(key, part):
    k_angle, k_long, k_wide, k_drift, k_rough = jax.random.split(key, 5)
    angle = jax.random.uniform(k_angle, (SPECIES, 1, 1), jnp.float32, -math.pi, math.pi)
    along_width = float(HALF) * jax.random.uniform(k_long, (SPECIES, 1, 1), jnp.float32, 0.3, 0.6)
    across_width = float(HALF) * jax.random.uniform(k_wide, (SPECIES, 1, 1), jnp.float32, 0.15, 0.3)
    drift = float(HALF) * jax.random.uniform(k_drift, (SPECIES, 1, 1), jnp.float32, -0.2, 0.2)
    offsets = jnp.arange(KW, dtype=jnp.float32) - float(HALF)
    first = offsets[None, :, None]
    second = offsets[None, None, :]
    along = jnp.cos(angle) * first + jnp.sin(angle) * second - drift
    across = -jnp.sin(angle) * first + jnp.cos(angle) * second
    envelope = jnp.exp(-0.5 * ((along / along_width) ** 2 + (across / across_width) ** 2)) + 0.05
    scale = 2.0 * math.pi * along_width * across_width + 0.05 * float(KW * KW)
    rough = jax.random.uniform(k_rough, (SPECIES, KW, KW), jnp.float32, 0.5, 1.5)
    return (envelope * rough / scale).astype(jnp.float32)


def steps_of(stream_key, extent, pieces, smallest, largest):
    gain, own = 1.0, jax.random.fold_in(stream_key, 6)
    for position, parts in pieces:
        steps = jnp.exp(jax.random.uniform(jax.random.fold_in(own, position), (parts,), jnp.float32, smallest / len(pieces), largest / len(pieces)))
        gain = gain * jnp.repeat(steps, extent[position] // parts).reshape([-1 if axis == position else 1 for axis in range(len(extent))])
    return gain


def setup_inputs(seed: int = 0) -> dict:
    streams_of = jax.random.split(jax.random.key(seed), 7)
    return {
        "emissions": draw_emissions(jax.random.fold_in(streams_of[6], 71), 0),
        "winds": jnp.clip(jax.random.uniform(streams_of[1], (STEPS, 2, NR, NC), jnp.float32, -0.4, 0.4) * steps_of(streams_of[1], (STEPS, 2, NR, NC), ((2, 8), (3, 4)), -0.4, 0.0), -0.4, 0.4),
        "kernels": draw_kernels(jax.random.fold_in(streams_of[6], 71), 0),
        "box_states": jnp.clip(jnp.exp(math.log(0.3) - 2.7080503 * jax.random.uniform(streams_of[3], (SPECIES, BOXES, NR, NC), jnp.float32) ** steps_of(streams_of[3], (SPECIES, BOXES, NR, NC), ((2, 8), (3, 4)), -0.2, 0.2)), 0.02, 0.3),
        "decay": jnp.clip(jax.random.uniform(streams_of[4], (SPECIES, BOXES), jnp.float32, 0.3, 0.95), 0.3, 0.95),
        "fraction": jnp.clip(jax.random.uniform(streams_of[5], (SPECIES, BOXES), jnp.float32, 0.1, 0.6), 0.1, 0.6),
    }


diffusion_number = 0.05


def disperse(emission, kernel):
    rows = emission.shape[-2] + kernel.shape[-2] - 1
    cols = emission.shape[-1] + kernel.shape[-1] - 1
    spectrum = jnp.fft.rfft2(emission, s=(rows, cols)) * jnp.fft.rfft2(kernel, s=(rows, cols))
    full = jnp.fft.irfft2(spectrum, s=(rows, cols))
    reach = (kernel.shape[-1] - 1) // 2
    return full[:, reach:reach + emission.shape[-2], reach:reach + emission.shape[-1]].astype(emission.dtype)


def transport(mixed, column_wind, row_wind):
    padded = jnp.pad(mixed, ((0, 0), (0, 0), (1, 1), (1, 1)))
    north = padded[:, :, :-2, 1:-1]
    south = padded[:, :, 2:, 1:-1]
    west = padded[:, :, 1:-1, :-2]
    east = padded[:, :, 1:-1, 2:]
    flow = jnp.maximum(column_wind, 0.0) * (mixed - west) + jnp.minimum(column_wind, 0.0) * (east - mixed)
    flow = flow + jnp.maximum(row_wind, 0.0) * (mixed - north) + jnp.minimum(row_wind, 0.0) * (south - mixed)
    return mixed - flow + diffusion_number * (north + south + east + west - 4.0 * mixed)


def reference(emissions, winds, kernels, box_states, decay, fraction):
    state = box_states
    for hour in range(STEPS):
        source = disperse(emissions[hour], kernels)
        mixed = decay[:, :, None, None] * state + fraction[:, :, None, None] * source[:, None]
        state = transport(mixed, winds[hour, 0], winds[hour, 1])
    return state, jnp.sum(state, axis=1)
```

```python
import functools
import math

import jax
import jax.numpy as jnp
import numpy as np
from jax import lax
from jax.experimental import pallas as pl
from jax.experimental.pallas import tpu as pltpu
from jax.sharding import PartitionSpec as P

STEPS = 2
DIFFUSION = 0.05
MESH = pl.DeviceIdType.MESH
F32 = jnp.float32
BF16 = jnp.bfloat16


def split_table(table):
    high = table.astype(jnp.bfloat16)
    low = (table - high.astype(np.float64)).astype(jnp.bfloat16)
    return np.stack([high, low])


def tables(tile, reach, lanes):
    period = 2 * tile
    freq = (np.arange(tile) + 0.5) * (2.0 * math.pi / period)
    own = np.arange(tile)
    before = np.arange(-reach, 0)
    after = np.arange(tile, tile + reach)
    centred = np.arange(-reach, reach + 1)

    def forward_cols(positions):
        angle = positions[:, None] * freq[None, :]
        return np.concatenate([np.cos(angle), -np.sin(angle)], axis=1)

    def forward_rows(positions):
        angle = freq[:, None] * positions[None, :]
        return np.concatenate([np.cos(angle), np.sin(angle)], axis=0)

    cols_a = forward_cols(np.concatenate([own, before, before, after, after]))
    cols_b = forward_cols(np.concatenate([own, after, after, before, before]))
    rows_f = forward_rows(np.concatenate([own, before, after]))
    kernel_cols = np.zeros((lanes, 2 * tile))
    kernel_cols[: centred.size] = forward_cols(centred) * (2.0 / period**2)
    kernel_rows = np.zeros((2 * tile, lanes))
    kernel_rows[:, : centred.size] = forward_rows(centred)
    angle = own[:, None] * freq[None, :]
    rows_i = np.concatenate([np.cos(angle), np.sin(angle)], axis=1)
    cols_i = np.concatenate([np.cos(angle).T, -np.sin(angle).T], axis=0)
    return [split_table(t) for t in (cols_a, cols_b, rows_f, kernel_cols, kernel_rows, rows_i, cols_i)]


def split(value):
    high = value.astype(BF16)
    low = (value - high.astype(F32)).astype(BF16)
    return high, low


def dot3(left, right):
    lh, ll = left
    rh, rl = right
    return (
        jnp.dot(lh, rh, preferred_element_type=F32)
        + jnp.dot(ll, rh, preferred_element_type=F32)
        + jnp.dot(lh, rl, preferred_element_type=F32)
    )


def kernel(
    rows, cols, tile, reach,
    em, wd, kern, bs, decay, fraction,
    t_ca, t_cb, t_rf, t_ck, t_kr, t_ri, t_ci,
    out, surf,
    e_v, w_v, s_v,
    v_ca, v_cb, v_rf, v_ck, v_kr, v_ri, v_ci,
    kpad, kspec, send_e, send_w, west, east, ns, xh, xl, mix, src,
    n_send, s_send, n_recv, s_recv, c_send, w_recv, e_recv,
    coef,
    lsem, ssem, rsem,
):
    species = e_v.shape[1]
    boxes = s_v.shape[1]
    r = lax.axis_index("row")
    c = lax.axis_index("col")
    has = {"n": r > 0, "s": r < rows - 1, "w": c > 0, "e": c < cols - 1}
    dev = {
        "n": (jnp.maximum(r - 1, 0), c),
        "s": (jnp.minimum(r + 1, rows - 1), c),
        "w": (r, jnp.maximum(c - 1, 0)),
        "e": (r, jnp.minimum(c + 1, cols - 1)),
    }
    opposite = {"n": "s", "s": "n", "w": "e", "e": "w"}
    sends = []

    barrier = pltpu.get_barrier_semaphore()
    for side in "nswe":
        @pl.when(has[side])
        def _():
            pl.semaphore_signal(barrier, inc=1, device_id=dev[side], device_id_type=MESH)

    local = []

    def load(source, target):
        copy = pltpu.make_async_copy(source, target, lsem.at[len(local)])
        copy.start()
        local.append(copy)
        return copy

    load_e = [load(em.at[t], e_v.at[t]) for t in range(STEPS)]
    load_k = [load(a, b) for a, b in ((t_ck, v_ck), (t_kr, v_kr))]
    load_t = [
        load(a, b)
        for a, b in ((t_ca, v_ca), (t_cb, v_cb), (t_rf, v_rf), (t_ri, v_ri), (t_ci, v_ci))
    ]
    load_w = load(wd, w_v)
    load_s = load(bs, s_v)

    def remote(channel, side, source, target):
        return pltpu.make_async_remote_copy(
            src_ref=source,
            dst_ref=target,
            send_sem=ssem.at[channel],
            recv_sem=rsem.at[channel],
            device_id=dev[side],
            device_id_type=MESH,
        )

    def send(channel, side, source, target):
        @pl.when(has[side])
        def _():
            remote(channel, side, source, target).start()

        sends.append((channel, side, source, target))

    def wait_recv(channel, side, source, target):
        @pl.when(has[opposite[side]])
        def _():
            remote(channel, side, source, target).wait_recv()

    @pl.when(jnp.logical_not(has["n"]))
    def _():
        ns[:, :, :reach, :] = jnp.zeros((STEPS, species, reach, tile), F32)
        west[:, tile : tile + reach, :] = jnp.zeros((STEPS, reach, tile), F32)
        east[:, tile : tile + reach, :] = jnp.zeros((STEPS, reach, tile), F32)
        n_recv[...] = jnp.zeros(n_recv.shape, F32)

    @pl.when(jnp.logical_not(has["s"]))
    def _():
        ns[:, :, reach:, :] = jnp.zeros((STEPS, species, reach, tile), F32)
        west[:, tile + reach :, :] = jnp.zeros((STEPS, reach, tile), F32)
        east[:, tile + reach :, :] = jnp.zeros((STEPS, reach, tile), F32)
        s_recv[...] = jnp.zeros(s_recv.shape, F32)

    @pl.when(jnp.logical_not(has["w"]))
    def _():
        west[:, :tile, :] = jnp.zeros((STEPS, tile, tile), F32)
        w_recv[...] = jnp.zeros(w_recv.shape, F32)

    @pl.when(jnp.logical_not(has["e"]))
    def _():
        east[:, :tile, :] = jnp.zeros((STEPS, tile, tile), F32)
        e_recv[...] = jnp.zeros(e_recv.shape, F32)

    lane = lax.broadcasted_iota(jnp.int32, (tile, tile), 1)
    row = lax.broadcasted_iota(jnp.int32, (tile, tile), 0)
    slot = lane // reach
    own_rows = pl.ds(0, tile)

    def strip_args(t):
        return (
            (8 * t + 0, "e", send_e.at[t], west.at[t, own_rows]),
            (8 * t + 1, "w", send_w.at[t], east.at[t, own_rows]),
        )

    def row_args(t):
        return (
            (8 * t + 2, "s", em.at[t, :, pl.ds(tile - reach, reach), :], ns.at[t, :, pl.ds(0, reach), :]),
            (8 * t + 3, "n", em.at[t, :, pl.ds(0, reach), :], ns.at[t, :, pl.ds(reach, reach), :]),
        )

    def corner_args(t):
        found = []
        for position, strip in enumerate((west, east)):
            found.append(
                (8 * t + 4 + 2 * position, "s", strip.at[t, pl.ds(tile - reach, reach)], strip.at[t, pl.ds(tile, reach)])
            )
            found.append(
                (8 * t + 5 + 2 * position, "n", strip.at[t, pl.ds(0, reach)], strip.at[t, pl.ds(tile + reach, reach)])
            )
        return found

    for t in range(STEPS):
        load_e[t].wait()
        for target, first, turn in ((send_e, tile - reach, 0), (send_w, 0, 2)):
            packed = None
            for s in range(species):
                place = (s + turn) % species
                moved = pltpu.roll(e_v[t, s], (reach * place - first) % tile, 1)
                packed = moved if packed is None else jnp.where(slot == place, moved, packed)
            target[t] = packed
        if t == 0:
            peers = sum(has[side].astype(jnp.int32) for side in "nswe")
            pl.semaphore_wait(barrier, peers)
        for args in strip_args(t) + row_args(t):
            send(*args)

    kpad[...] = jnp.zeros(kpad.shape, F32)
    width = 2 * reach + 1
    for s in range(species):
        kpad[s, :width, :width] = kern[:, s, :]
    for copy in load_k:
        copy.wait()
    def even_odd(value):
        u, w = value[:tile, :tile], value[:tile, tile:]
        z, v = value[tile:, :tile], value[tile:, tile:]
        return u + v, w - z, u - v, w + z

    for s in range(species):
        first = dot3(split(kpad[s]), (v_ck[0], v_ck[1]))
        second = dot3((v_kr[0], v_kr[1]), split(first))
        for position, value in enumerate(even_odd(second)):
            kspec[s, position] = value

    def own_part(t):
        for s in range(species):
            high, low = split(e_v[t, s])
            xh[s, :tile, :tile] = high
            xl[s, :tile, :tile] = low

    def rows_part(t):
        for s in range(species):
            high, low = split(ns[t, s])
            xh[s, tile:, :tile] = high
            xl[s, tile:, :tile] = low

    def cols_part(t):
        wide = lax.broadcasted_iota(jnp.int32, (tile + 2 * reach, tile), 1)
        from_west, from_east = west[t], east[t]
        left = wide < tile // 2
        for pair in range(2):
            joined = jnp.where(left, from_west, from_east) if pair == 0 else jnp.where(left, from_east, from_west)
            for odd in range(2):
                s = 2 * pair + odd
                mine = jnp.where((wide // reach) % 2 == odd, joined, 0.0)
                high, low = split(mine)
                xh[s, :, tile:] = high
                xl[s, :, tile:] = low

    def disperse(t):
        for s in range(species):
            table = v_ca if s < 2 else v_cb
            a = dot3((xh[s], xl[s]), (table[0], table[1]))
            b = dot3((v_rf[0], v_rf[1]), split(a))
            pr, pi, mr, mi = even_odd(b)
            kpr, kpi, kmr, kmi = (kspec[s, n] for n in range(4))
            gpr = pr * kpr - pi * kpi
            gpi = pr * kpi + pi * kpr
            gmr = mr * kmr - mi * kmi
            gmi = mr * kmi + mi * kmr
            top = jnp.concatenate([gpr + gmr, gpi + gmi], axis=1)
            bottom = jnp.concatenate([gmi - gpi, gpr - gmr], axis=1)
            g = jnp.concatenate([top, bottom], axis=0)
            d = dot3((v_ri[0], v_ri[1]), split(g))
            src[t, s] = dot3(split(d), (v_ci[0], v_ci[1]))

    first_row = 8
    inner = pl.ds(first_row, tile)
    packed_rows = c_send.shape[1]

    def edge_args(t):
        base = 16 + 4 * t
        return (
            (base + 0, "n", n_send.at[t], s_recv.at[t]),
            (base + 1, "s", s_send.at[t], n_recv.at[t]),
            (base + 2, "w", c_send.at[t], e_recv.at[t]),
            (base + 3, "e", c_send.at[t], w_recv.at[t]),
        )

    def mix_and_send(t, state):
        packed = jnp.zeros((tile, tile), F32)
        for s in range(species):
            for k in range(boxes):
                f = s * boxes + k
                m = decay[s, k] * state[s, k] + fraction[s, k] * src[t, s]
                mix[f, inner, :] = m
                n_send[t, f : f + 1, :] = m[0:1, :]
                s_send[t, f : f + 1, :] = m[tile - 1 : tile, :]
                packed = jnp.where(lane // 2 == f, pltpu.roll(m, 2 * f + 1, 1), packed)
        c_send[t] = packed.T[:packed_rows]
        for args in edge_args(t):
            send(*args)

    def coefficients(t):
        u, v = w_v[t, 0], w_v[t, 1]
        up, um = jnp.maximum(u, 0.0), jnp.minimum(u, 0.0)
        vp, vm = jnp.maximum(v, 0.0), jnp.minimum(v, 0.0)
        coef[0] = (1.0 - 4.0 * DIFFUSION) - up + um - vp + vm
        to_west, to_east = up + DIFFUSION, DIFFUSION - um
        coef[1] = jnp.where(lane > 0, to_west, 0.0)
        coef[2] = jnp.where(lane < tile - 1, to_east, 0.0)
        coef[3] = vp + DIFFUSION
        coef[4] = DIFFUSION - vm
        coef[5] = jnp.where(lane == 0, to_west, jnp.where(lane == tile - 1, to_east, 0.0))

    def transport(t, result):
        for args in edge_args(t):
            wait_recv(*args)
        for f in range(species * boxes):
            mix[f, first_row - 1 : first_row, :] = n_recv[t, f : f + 1, :]
            mix[f, first_row + tile : first_row + tile + 1, :] = s_recv[t, f : f + 1, :]
        odd = lax.broadcasted_iota(jnp.int32, (packed_rows, tile), 0) % 2 == 1
        joined = jnp.where(
            odd, pltpu.roll(w_recv[t], 1, 0), pltpu.roll(e_recv[t], packed_rows - 1, 0)
        )
        joined = jnp.concatenate([joined, jnp.zeros((tile - packed_rows, tile), F32)], axis=0)
        beside = joined.T
        for s in range(species):
            total = None
            for k in range(boxes):
                f = s * boxes + k
                m = mix[f, inner, :]
                value = (
                    coef[0] * m
                    + coef[1] * pltpu.roll(m, 1, 1)
                    + coef[2] * pltpu.roll(m, tile - 1, 1)
                    + coef[3] * mix[f, pl.ds(first_row - 1, tile), :]
                    + coef[4] * mix[f, pl.ds(first_row + 1, tile), :]
                    + coef[5] * pltpu.roll(beside, (tile - 2 * f - 1) % tile, 1)
                )
                result[s, k] = value
                total = value if total is None else total + value
            if t == STEPS - 1:
                surf[s] = total

    def arrive(t):
        for args in strip_args(t):
            wait_recv(*args)
        for args in corner_args(t):
            send(*args)

    def source(t):
        own_part(t)
        for args in row_args(t):
            wait_recv(*args)
        rows_part(t)
        for args in corner_args(t):
            wait_recv(*args)
        cols_part(t)
        disperse(t)

    arrive(0)
    for copy in load_t:
        copy.wait()
    source(0)
    arrive(1)
    load_s.wait()
    load_w.wait()
    mix_and_send(0, s_v)
    source(1)
    coefficients(0)
    transport(0, s_v)
    mix_and_send(1, s_v)
    coefficients(1)
    transport(1, out)
    for channel, side, sent, target in sends:
        @pl.when(has[side])
        def _():
            remote(channel, side, sent, target).wait_send()


def on_device(rows, cols, emissions, winds, kernels, box_states, decay, fraction):
    _, species, tile, _ = emissions.shape
    boxes = box_states.shape[1]
    reach = (kernels.shape[-1] - 1) // 2
    fields = species * boxes
    tabs = [jnp.asarray(t) for t in tables(tile, reach, tile)]
    hbm = pl.BlockSpec(memory_space=pltpu.HBM)
    vmem = pl.BlockSpec(memory_space=pltpu.VMEM)
    smem = pl.BlockSpec(memory_space=pltpu.SMEM)
    span = tile + 2 * reach

    def buf(*shape, dtype=F32):
        return pltpu.VMEM(shape, dtype)

    channels = 16 + 4 * STEPS
    return tuple(
        pl.pallas_call(
            functools.partial(kernel, rows, cols, tile, reach),
            out_shape=(
                jax.ShapeDtypeStruct(box_states.shape, F32),
                jax.ShapeDtypeStruct((species, tile, tile), F32),
            ),
            in_specs=[hbm, hbm, vmem, hbm, smem, smem] + [hbm] * len(tabs),
            out_specs=(vmem, vmem),
            scratch_shapes=[
                buf(STEPS, species, tile, tile),
                buf(STEPS, 2, tile, tile),
                buf(species, boxes, tile, tile),
            ]
            + [buf(*t.shape, dtype=BF16) for t in tabs]
            + [
                buf(species, tile, tile),
                buf(species, 4, tile, tile),
                buf(STEPS, tile, tile),
                buf(STEPS, tile, tile),
                buf(STEPS, span, tile),
                buf(STEPS, span, tile),
                buf(STEPS, species, 2 * reach, tile),
                buf(species, span, 2 * tile, dtype=BF16),
                buf(species, span, 2 * tile, dtype=BF16),
                buf(fields, tile + 16, tile),
                buf(STEPS, species, tile, tile),
                buf(STEPS, fields, tile),
                buf(STEPS, fields, tile),
                buf(STEPS, fields, tile),
                buf(STEPS, fields, tile),
                buf(STEPS, 2 * fields, tile),
                buf(STEPS, 2 * fields, tile),
                buf(STEPS, 2 * fields, tile),
                buf(6, tile, tile),
                pltpu.SemaphoreType.DMA((STEPS + len(tabs) + 2,)),
                pltpu.SemaphoreType.DMA((channels,)),
                pltpu.SemaphoreType.DMA((channels,)),
            ],
            compiler_params=pltpu.CompilerParams(
                collective_id=0, has_side_effects=True, vmem_limit_bytes=61 * 2**20
            ),
        )(emissions, winds, kernels.transpose(1, 0, 2), box_states, decay, fraction, *tabs)
    )


def solution(mesh):
    placed = (
        P(None, None, "row", "col"),
        P(None, None, "row", "col"),
        P(),
        P(None, None, "row", "col"),
        P(),
        P(),
    )
    return jax.shard_map(
        functools.partial(on_device, mesh.shape["row"], mesh.shape["col"]),
        mesh=mesh,
        in_specs=placed,
        out_specs=(P(None, None, "row", "col"), P(None, "row", "col")),
        check_vma=False,
    )
```

```python
import functools
import math

import jax
import jax.numpy as jnp
import numpy as np
from jax import lax
from jax.experimental import pallas as pl
from jax.experimental.pallas import tpu as pltpu
from jax.sharding import PartitionSpec as P

STEPS = 2
DIFFUSION = 0.05
MESH = pl.DeviceIdType.MESH
F32 = jnp.float32
BF16 = jnp.bfloat16


def split_table(table):
    high = table.astype(jnp.bfloat16)
    low = (table - high.astype(np.float64)).astype(jnp.bfloat16)
    return np.stack([high, low])


def tables(tile, reach, lanes):
    period = 2 * tile
    freq = (np.arange(tile) + 0.5) * (2.0 * math.pi / period)
    own = np.arange(tile)
    before = np.arange(-reach, 0)
    after = np.arange(tile, tile + reach)
    centred = np.arange(-reach, reach + 1)

    def forward_cols(positions):
        angle = positions[:, None] * freq[None, :]
        return np.concatenate([np.cos(angle), -np.sin(angle)], axis=1)

    def forward_rows(positions):
        angle = freq[:, None] * positions[None, :]
        return np.concatenate([np.cos(angle), np.sin(angle)], axis=0)

    cols_a = forward_cols(np.concatenate([own, before, before, after, after]))
    cols_b = forward_cols(np.concatenate([own, after, after, before, before]))
    rows_f = forward_rows(np.concatenate([own, before, after]))
    kernel_cols = np.zeros((lanes, 2 * tile))
    kernel_cols[: centred.size] = forward_cols(centred) * (2.0 / period**2)
    kernel_rows = np.zeros((2 * tile, lanes))
    kernel_rows[:, : centred.size] = forward_rows(centred)
    angle = own[:, None] * freq[None, :]
    rows_i = np.concatenate([np.cos(angle), np.sin(angle)], axis=1)
    cols_i = np.concatenate([np.cos(angle).T, -np.sin(angle).T], axis=0)
    return [split_table(t) for t in (cols_a, cols_b, rows_f, kernel_cols, kernel_rows, rows_i, cols_i)]


def split(value):
    high = value.astype(BF16)
    low = (value - high.astype(F32)).astype(BF16)
    return high, low


def dot3(left, right):
    lh, ll = left
    rh, rl = right
    return (
        jnp.dot(lh, rh, preferred_element_type=F32)
        + jnp.dot(ll, rh, preferred_element_type=F32)
        + jnp.dot(lh, rl, preferred_element_type=F32)
    )


def kernel(
    rows, cols, tile, reach,
    em, wd, kern, bs, decay, fraction,
    t_ca, t_cb, t_rf, t_ck, t_kr, t_ri, t_ci,
    out, surf,
    e_v, w_v, s_v, k_v,
    v_ca, v_cb, v_rf, v_ck, v_kr, v_ri, v_ci,
    kpad, kspec, send_e, send_w, west, east, ns, xh, xl, mix, src,
    n_send, s_send, n_recv, s_recv, c_send, w_recv, e_recv,
    coef,
    lsem, ssem, rsem,
):
    species = e_v.shape[1]
    boxes = s_v.shape[1]
    r = lax.axis_index("row")
    c = lax.axis_index("col")
    has = {"n": r > 0, "s": r < rows - 1, "w": c > 0, "e": c < cols - 1}
    up, down = jnp.maximum(r - 1, 0), jnp.minimum(r + 1, rows - 1)
    left, right = jnp.maximum(c - 1, 0), jnp.minimum(c + 1, cols - 1)
    dev = {"n": (up, c), "s": (down, c), "w": (r, left), "e": (r, right)}
    dev |= {"nw": (up, left), "ne": (up, right), "sw": (down, left), "se": (down, right)}
    for side in ("nw", "ne", "sw", "se"):
        has[side] = jnp.logical_and(has[side[0]], has[side[1]])
    opposite = {"n": "s", "s": "n", "w": "e", "e": "w", "nw": "se", "se": "nw", "ne": "sw", "sw": "ne"}
    sends = []

    barrier = pltpu.get_barrier_semaphore()
    for side in has:
        @pl.when(has[side])
        def _():
            pl.semaphore_signal(barrier, inc=1, device_id=dev[side], device_id_type=MESH)

    local = []

    def load(source, target):
        copy = pltpu.make_async_copy(source, target, lsem.at[len(local)])
        copy.start()
        local.append(copy)
        return copy

    load_e = [load(em.at[t], e_v.at[t]) for t in range(STEPS)]
    load_k = [load(a, b) for a, b in ((kern, k_v), (t_ck, v_ck), (t_kr, v_kr))]
    load_t = [
        load(a, b)
        for a, b in ((t_ca, v_ca), (t_cb, v_cb), (t_rf, v_rf), (t_ri, v_ri), (t_ci, v_ci))
    ]
    load_w = load(wd, w_v)
    load_s = load(bs, s_v)

    def remote(channel, side, source, target):
        return pltpu.make_async_remote_copy(
            src_ref=source,
            dst_ref=target,
            send_sem=ssem.at[channel],
            recv_sem=rsem.at[channel],
            device_id=dev[side],
            device_id_type=MESH,
        )

    def send(channel, side, source, target):
        @pl.when(has[side])
        def _():
            remote(channel, side, source, target).start()

        sends.append((channel, side, source, target))

    def wait_recv(channel, side, source, target):
        @pl.when(has[opposite[side]])
        def _():
            remote(channel, side, source, target).wait_recv()

    @pl.when(jnp.logical_not(has["n"]))
    def _():
        ns[:, :, :reach, :] = jnp.zeros((STEPS, species, reach, tile), F32)
        n_recv[...] = jnp.zeros(n_recv.shape, F32)

    @pl.when(jnp.logical_not(has["s"]))
    def _():
        ns[:, :, reach:, :] = jnp.zeros((STEPS, species, reach, tile), F32)
        s_recv[...] = jnp.zeros(s_recv.shape, F32)

    @pl.when(jnp.logical_not(has["w"]))
    def _():
        west[:, :tile, :] = jnp.zeros((STEPS, tile, tile), F32)
        w_recv[...] = jnp.zeros(w_recv.shape, F32)

    @pl.when(jnp.logical_not(has["e"]))
    def _():
        east[:, :tile, :] = jnp.zeros((STEPS, tile, tile), F32)
        e_recv[...] = jnp.zeros(e_recv.shape, F32)

    for side, strip, first in (
        ("nw", west, tile), ("sw", west, tile + reach), ("ne", east, tile), ("se", east, tile + reach)
    ):
        @pl.when(jnp.logical_not(has[side]))
        def _():
            strip[:, first : first + reach, :] = jnp.zeros((STEPS, reach, tile), F32)

    lane = lax.broadcasted_iota(jnp.int32, (tile, tile), 1)
    row = lax.broadcasted_iota(jnp.int32, (tile, tile), 0)
    slot = lane // reach
    own_rows = pl.ds(0, tile)

    def strip_args(t):
        return (
            (8 * t + 0, "e", send_e.at[t], west.at[t, own_rows]),
            (8 * t + 1, "w", send_w.at[t], east.at[t, own_rows]),
        )

    def row_args(t):
        return (
            (8 * t + 2, "s", em.at[t, :, pl.ds(tile - reach, reach), :], ns.at[t, :, pl.ds(0, reach), :]),
            (8 * t + 3, "n", em.at[t, :, pl.ds(0, reach), :], ns.at[t, :, pl.ds(reach, reach), :]),
        )

    def corner_args(t):
        top, bottom = pl.ds(0, reach), pl.ds(tile - reach, reach)
        before, after = pl.ds(tile, reach), pl.ds(tile + reach, reach)
        return (
            (8 * t + 4, "se", send_e.at[t, bottom], west.at[t, before]),
            (8 * t + 5, "ne", send_e.at[t, top], west.at[t, after]),
            (8 * t + 6, "sw", send_w.at[t, bottom], east.at[t, before]),
            (8 * t + 7, "nw", send_w.at[t, top], east.at[t, after]),
        )

    for t in range(STEPS):
        load_e[t].wait()
        for target, first, turn in ((send_e, tile - reach, 0), (send_w, 0, 2)):
            packed = None
            for s in range(species):
                place = (s + turn) % species
                moved = pltpu.roll(e_v[t, s], (reach * place - first) % tile, 1)
                packed = moved if packed is None else jnp.where(slot == place, moved, packed)
            target[t] = packed
        if t == 0:
            peers = sum(has[side].astype(jnp.int32) for side in has)
            pl.semaphore_wait(barrier, peers)
        for args in strip_args(t) + corner_args(t) + row_args(t):
            send(*args)

    kpad[...] = jnp.zeros(kpad.shape, F32)
    width = 2 * reach + 1
    for copy in load_k:
        copy.wait()
    for s in range(species):
        kpad[s, :width, :width] = k_v[:, s, :]
    def even_odd(value):
        u, w = value[:tile, :tile], value[:tile, tile:]
        z, v = value[tile:, :tile], value[tile:, tile:]
        return u + v, w - z, u - v, w + z

    for s in range(species):
        first = dot3(split(kpad[s]), (v_ck[0], v_ck[1]))
        second = dot3((v_kr[0], v_kr[1]), split(first))
        for position, value in enumerate(even_odd(second)):
            kspec[s, position] = value

    def own_part(t):
        for s in range(species):
            high, low = split(e_v[t, s])
            xh[s, :tile, :tile] = high
            xl[s, :tile, :tile] = low

    def rows_part(t):
        for s in range(species):
            high, low = split(ns[t, s])
            xh[s, tile:, :tile] = high
            xl[s, tile:, :tile] = low

    def cols_part(t):
        wide = lax.broadcasted_iota(jnp.int32, (tile + 2 * reach, tile), 1)
        from_west, from_east = west[t], east[t]
        left = wide < tile // 2
        for pair in range(2):
            joined = jnp.where(left, from_west, from_east) if pair == 0 else jnp.where(left, from_east, from_west)
            for odd in range(2):
                s = 2 * pair + odd
                mine = jnp.where((wide // reach) % 2 == odd, joined, 0.0)
                high, low = split(mine)
                xh[s, :, tile:] = high
                xl[s, :, tile:] = low

    def disperse(t):
        span = tile + 2 * reach
        firsts = []
        for pair, table in enumerate((v_ca, v_cb)):
            both = pl.ds(2 * pair, 2)
            x = tuple(ref[both].reshape(2 * span, 2 * tile) for ref in (xh, xl))
            a = dot3(x, (table[0], table[1]))
            firsts += [split(a[:span]), split(a[span:])]
        seconds = [dot3((v_rf[0], v_rf[1]), a) for a in firsts]
        spectra = []
        for s in range(species):
            pr, pi, mr, mi = even_odd(seconds[s])
            kpr, kpi, kmr, kmi = (kspec[s, n] for n in range(4))
            gpr = pr * kpr - pi * kpi
            gpi = pr * kpi + pi * kpr
            gmr = mr * kmr - mi * kmi
            gmi = mr * kmi + mi * kmr
            top = jnp.concatenate([gpr + gmr, gpi + gmi], axis=1)
            bottom = jnp.concatenate([gmi - gpi, gpr - gmr], axis=1)
            spectra.append(split(jnp.concatenate([top, bottom], axis=0)))
        thirds = [split(dot3((v_ri[0], v_ri[1]), g)) for g in spectra]
        for s in range(species):
            src[t, s] = dot3(thirds[s], (v_ci[0], v_ci[1]))

    first_row = 8
    inner = pl.ds(first_row, tile)
    packed_rows = c_send.shape[1]

    def edge_args(t):
        base = 16 + 4 * t
        return (
            (base + 0, "n", n_send.at[t], s_recv.at[t]),
            (base + 1, "s", s_send.at[t], n_recv.at[t]),
            (base + 2, "w", c_send.at[t], e_recv.at[t]),
            (base + 3, "e", c_send.at[t], w_recv.at[t]),
        )

    def mix_and_send(t, state):
        packed = jnp.zeros((tile, tile), F32)
        for s in range(species):
            for k in range(boxes):
                f = s * boxes + k
                m = decay[s, k] * state[s, k] + fraction[s, k] * src[t, s]
                mix[f, inner, :] = m
                n_send[t, f : f + 1, :] = m[0:1, :]
                s_send[t, f : f + 1, :] = m[tile - 1 : tile, :]
                packed = jnp.where(lane // 2 == f, pltpu.roll(m, 2 * f + 1, 1), packed)
        c_send[t] = packed.T[:packed_rows]
        for args in edge_args(t):
            send(*args)

    def coefficients(t):
        u, v = w_v[t, 0], w_v[t, 1]
        up, um = jnp.maximum(u, 0.0), jnp.minimum(u, 0.0)
        vp, vm = jnp.maximum(v, 0.0), jnp.minimum(v, 0.0)
        coef[0] = (1.0 - 4.0 * DIFFUSION) - up + um - vp + vm
        to_west, to_east = up + DIFFUSION, DIFFUSION - um
        coef[1] = jnp.where(lane > 0, to_west, 0.0)
        coef[2] = jnp.where(lane < tile - 1, to_east, 0.0)
        coef[3] = vp + DIFFUSION
        coef[4] = DIFFUSION - vm
        coef[5] = jnp.where(lane == 0, to_west, jnp.where(lane == tile - 1, to_east, 0.0))

    def stencil(f):
        m = mix[f, inner, :]
        return (
            coef[0] * m
            + coef[1] * pltpu.roll(m, 1, 1)
            + coef[2] * pltpu.roll(m, tile - 1, 1)
            + coef[3] * mix[f, pl.ds(first_row - 1, tile), :]
            + coef[4] * mix[f, pl.ds(first_row + 1, tile), :]
        )

    def beside(t):
        odd = lax.broadcasted_iota(jnp.int32, (packed_rows, tile), 0) % 2 == 1
        joined = jnp.where(
            odd, pltpu.roll(w_recv[t], 1, 0), pltpu.roll(e_recv[t], packed_rows - 1, 0)
        )
        return jnp.concatenate([joined, jnp.zeros((tile - packed_rows, tile), F32)], axis=0).T

    def from_sides(halo, f):
        return coef[5] * pltpu.roll(halo, (tile - 2 * f - 1) % tile, 1)

    def transport_first(t, result):
        for args in edge_args(t):
            wait_recv(*args)
        for f in range(species * boxes):
            mix[f, first_row - 1 : first_row, :] = n_recv[t, f : f + 1, :]
            mix[f, first_row + tile : first_row + tile + 1, :] = s_recv[t, f : f + 1, :]
        halo = beside(t)
        for f in range(species * boxes):
            result[f // boxes, f % boxes] = stencil(f) + from_sides(halo, f)

    def transport_last(t, result, total):
        north, south = coef[3, 0:1, :], coef[4, tile - 1 : tile, :]
        coef[3] = jnp.where(row > 0, coef[3], 0.0)
        coef[4] = jnp.where(row < tile - 1, coef[4], 0.0)
        for f in range(species * boxes):
            result[f // boxes, f % boxes] = stencil(f)
        for args in edge_args(t):
            wait_recv(*args)
        halo = beside(t)
        for s in range(species):
            for k in range(boxes):
                f = s * boxes + k
                result[s, k, 0:1, :] += north * n_recv[t, f : f + 1, :]
                result[s, k, tile - 1 : tile, :] += south * s_recv[t, f : f + 1, :]
            summed = None
            for k in range(boxes):
                value = result[s, k] + from_sides(halo, s * boxes + k)
                result[s, k] = value
                summed = value if summed is None else summed + value
            total[s] = summed

    def source(t):
        own_part(t)
        for args in row_args(t):
            wait_recv(*args)
        rows_part(t)
        for args in strip_args(t) + corner_args(t):
            wait_recv(*args)
        cols_part(t)
        disperse(t)

    for copy in load_t:
        copy.wait()
    source(0)
    load_s.wait()
    load_w.wait()
    mix_and_send(0, s_v)
    source(1)
    coefficients(0)
    transport_first(0, s_v)
    mix_and_send(1, s_v)
    coefficients(1)
    transport_last(1, out, surf)
    for channel, side, sent, target in sends:
        @pl.when(has[side])
        def _():
            remote(channel, side, sent, target).wait_send()


def on_device(rows, cols, emissions, winds, kernels, box_states, decay, fraction):
    _, species, tile, _ = emissions.shape
    boxes = box_states.shape[1]
    reach = (kernels.shape[-1] - 1) // 2
    fields = species * boxes
    tabs = [jnp.asarray(t) for t in tables(tile, reach, tile)]
    hbm = pl.BlockSpec(memory_space=pltpu.HBM)
    vmem = pl.BlockSpec(memory_space=pltpu.VMEM)
    smem = pl.BlockSpec(memory_space=pltpu.SMEM)
    span = tile + 2 * reach

    def buf(*shape, dtype=F32):
        return pltpu.VMEM(shape, dtype)

    channels = 16 + 4 * STEPS
    return tuple(
        pl.pallas_call(
            functools.partial(kernel, rows, cols, tile, reach),
            out_shape=(
                jax.ShapeDtypeStruct(box_states.shape, F32),
                jax.ShapeDtypeStruct((species, tile, tile), F32),
            ),
            in_specs=[hbm, hbm, hbm, hbm, smem, smem] + [hbm] * len(tabs),
            out_specs=(vmem, vmem),
            scratch_shapes=[
                buf(STEPS, species, tile, tile),
                buf(STEPS, 2, tile, tile),
                buf(species, boxes, tile, tile),
                buf(2 * reach + 1, species, 2 * reach + 1),
            ]
            + [buf(*t.shape, dtype=BF16) for t in tabs]
            + [
                buf(species, tile, tile),
                buf(species, 4, tile, tile),
                buf(STEPS, tile, tile),
                buf(STEPS, tile, tile),
                buf(STEPS, span, tile),
                buf(STEPS, span, tile),
                buf(STEPS, species, 2 * reach, tile),
                buf(species, span, 2 * tile, dtype=BF16),
                buf(species, span, 2 * tile, dtype=BF16),
                buf(fields, tile + 16, tile),
                buf(STEPS, species, tile, tile),
                buf(STEPS, fields, tile),
                buf(STEPS, fields, tile),
                buf(STEPS, fields, tile),
                buf(STEPS, fields, tile),
                buf(STEPS, 2 * fields, tile),
                buf(STEPS, 2 * fields, tile),
                buf(STEPS, 2 * fields, tile),
                buf(6, tile, tile),
                pltpu.SemaphoreType.DMA((STEPS + len(tabs) + 3,)),
                pltpu.SemaphoreType.DMA((channels,)),
                pltpu.SemaphoreType.DMA((channels,)),
            ],
            compiler_params=pltpu.CompilerParams(
                collective_id=0, has_side_effects=True, vmem_limit_bytes=61 * 2**20
            ),
        )(emissions, winds, kernels.transpose(1, 0, 2), box_states, decay, fraction, *tabs)
    )


def solution(mesh):
    placed = (
        P(None, None, "row", "col"),
        P(None, None, "row", "col"),
        P(),
        P(None, None, "row", "col"),
        P(),
        P(),
    )
    return jax.shard_map(
        functools.partial(on_device, mesh.shape["row"], mesh.shape["col"]),
        mesh=mesh,
        in_specs=placed,
        out_specs=(P(None, None, "row", "col"), P(None, "row", "col")),
        check_vma=False,
    )
```

```python
import functools
import math

import jax
import jax.numpy as jnp
import numpy as np
from jax import lax
from jax.experimental import pallas as pl
from jax.experimental.pallas import tpu as pltpu
from jax.sharding import PartitionSpec as P

STEPS = 2
DIFFUSION = 0.05
MESH = pl.DeviceIdType.MESH
F32 = jnp.float32
BF16 = jnp.bfloat16


def split_table(table):
    high = table.astype(jnp.bfloat16)
    low = (table - high.astype(np.float64)).astype(jnp.bfloat16)
    return np.stack([high, low])


def tables(tile, reach, lanes):
    period = 2 * tile
    freq = (np.arange(tile) + 0.5) * (2.0 * math.pi / period)
    own = np.arange(tile)
    before = np.arange(-reach, 0)
    after = np.arange(tile, tile + reach)
    centred = np.arange(-reach, reach + 1)

    def forward_cols(positions):
        angle = positions[:, None] * freq[None, :]
        return np.concatenate([np.cos(angle), -np.sin(angle)], axis=1)

    def forward_rows(positions):
        angle = freq[:, None] * positions[None, :]
        return np.concatenate([np.cos(angle), np.sin(angle)], axis=0)

    cols_a = forward_cols(np.concatenate([own, before, before, after, after]))
    cols_b = forward_cols(np.concatenate([own, after, after, before, before]))
    rows_f = forward_rows(np.concatenate([own, before, after]))
    kernel_cols = np.zeros((lanes, 2 * tile))
    kernel_cols[: centred.size] = forward_cols(centred) * (2.0 / period**2)
    kernel_rows = np.zeros((2 * tile, lanes))
    kernel_rows[:, : centred.size] = forward_rows(centred)
    angle = own[:, None] * freq[None, :]
    rows_i = np.concatenate([np.cos(angle), np.sin(angle)], axis=1)
    cols_i = np.concatenate([np.cos(angle).T, -np.sin(angle).T], axis=0)
    return [split_table(t) for t in (cols_a, cols_b, rows_f, kernel_cols, kernel_rows, rows_i, cols_i)]


def split(value):
    high = value.astype(BF16)
    low = (value - high.astype(F32)).astype(BF16)
    return high, low


def dot3(left, right):
    lh, ll = left
    rh, rl = right
    return (
        jnp.dot(lh, rh, preferred_element_type=F32)
        + jnp.dot(ll, rh, preferred_element_type=F32)
        + jnp.dot(lh, rl, preferred_element_type=F32)
    )


def kernel(
    rows, cols, tile, reach,
    em, wd, kern, bs, decay, fraction,
    t_ca, t_cb, t_rf, t_ck, t_kr, t_ri, t_ci,
    part, side_halo, side_coef, row_halo,
    e_v, w_v, s_v, o_v, k_v,
    v_ca, v_cb, v_rf, v_ck, v_kr, v_ri, v_ci,
    kpad, kspec, send_e, send_w, west, east, ns, xh, xl, mix, src,
    n_send, s_send, n_recv, s_recv, c_send, w_recv, e_recv,
    coef,
    lsem, ssem, rsem, osem,
):
    species = e_v.shape[1]
    boxes = s_v.shape[1]
    r = lax.axis_index("row")
    c = lax.axis_index("col")
    has = {"n": r > 0, "s": r < rows - 1, "w": c > 0, "e": c < cols - 1}
    up, down = jnp.maximum(r - 1, 0), jnp.minimum(r + 1, rows - 1)
    left, right = jnp.maximum(c - 1, 0), jnp.minimum(c + 1, cols - 1)
    dev = {"n": (up, c), "s": (down, c), "w": (r, left), "e": (r, right)}
    dev |= {"nw": (up, left), "ne": (up, right), "sw": (down, left), "se": (down, right)}
    for side in ("nw", "ne", "sw", "se"):
        has[side] = jnp.logical_and(has[side[0]], has[side[1]])
    opposite = {"n": "s", "s": "n", "w": "e", "e": "w", "nw": "se", "se": "nw", "ne": "sw", "sw": "ne"}
    sends = []

    barrier = pltpu.get_barrier_semaphore()
    for side in has:
        @pl.when(has[side])
        def _():
            pl.semaphore_signal(barrier, inc=1, device_id=dev[side], device_id_type=MESH)

    local = []

    def load(source, target):
        copy = pltpu.make_async_copy(source, target, lsem.at[len(local)])
        copy.start()
        local.append(copy)
        return copy

    load_e = [load(em.at[t], e_v.at[t]) for t in range(STEPS)]
    load_k = [load(a, b) for a, b in ((kern, k_v), (t_ck, v_ck), (t_kr, v_kr))]
    load_t = [
        load(a, b)
        for a, b in ((t_ca, v_ca), (t_cb, v_cb), (t_rf, v_rf), (t_ri, v_ri), (t_ci, v_ci))
    ]
    load_w = load(wd, w_v)
    load_s = load(bs, s_v)

    def remote(channel, side, source, target):
        return pltpu.make_async_remote_copy(
            src_ref=source,
            dst_ref=target,
            send_sem=ssem.at[channel],
            recv_sem=rsem.at[channel],
            device_id=dev[side],
            device_id_type=MESH,
        )

    def send(channel, side, source, target):
        @pl.when(has[side])
        def _():
            remote(channel, side, source, target).start()

        sends.append((channel, side, source, target))

    def wait_recv(channel, side, source, target):
        @pl.when(has[opposite[side]])
        def _():
            remote(channel, side, source, target).wait_recv()

    @pl.when(jnp.logical_not(has["n"]))
    def _():
        ns[:, :, :reach, :] = jnp.zeros((STEPS, species, reach, tile), F32)
        n_recv[...] = jnp.zeros(n_recv.shape, F32)

    @pl.when(jnp.logical_not(has["s"]))
    def _():
        ns[:, :, reach:, :] = jnp.zeros((STEPS, species, reach, tile), F32)
        s_recv[...] = jnp.zeros(s_recv.shape, F32)

    @pl.when(jnp.logical_not(has["w"]))
    def _():
        west[:, :tile, :] = jnp.zeros((STEPS, tile, tile), F32)
        w_recv[...] = jnp.zeros(w_recv.shape, F32)

    @pl.when(jnp.logical_not(has["e"]))
    def _():
        east[:, :tile, :] = jnp.zeros((STEPS, tile, tile), F32)
        e_recv[...] = jnp.zeros(e_recv.shape, F32)

    for side, strip, first in (
        ("nw", west, tile), ("sw", west, tile + reach), ("ne", east, tile), ("se", east, tile + reach)
    ):
        @pl.when(jnp.logical_not(has[side]))
        def _():
            strip[:, first : first + reach, :] = jnp.zeros((STEPS, reach, tile), F32)

    lane = lax.broadcasted_iota(jnp.int32, (tile, tile), 1)
    row = lax.broadcasted_iota(jnp.int32, (tile, tile), 0)
    slot = lane // reach
    own_rows = pl.ds(0, tile)

    def strip_args(t):
        return (
            (8 * t + 0, "e", send_e.at[t], west.at[t, own_rows]),
            (8 * t + 1, "w", send_w.at[t], east.at[t, own_rows]),
        )

    def row_args(t):
        return (
            (8 * t + 2, "s", em.at[t, :, pl.ds(tile - reach, reach), :], ns.at[t, :, pl.ds(0, reach), :]),
            (8 * t + 3, "n", em.at[t, :, pl.ds(0, reach), :], ns.at[t, :, pl.ds(reach, reach), :]),
        )

    def corner_args(t):
        top, bottom = pl.ds(0, reach), pl.ds(tile - reach, reach)
        before, after = pl.ds(tile, reach), pl.ds(tile + reach, reach)
        return (
            (8 * t + 4, "se", send_e.at[t, bottom], west.at[t, before]),
            (8 * t + 5, "ne", send_e.at[t, top], west.at[t, after]),
            (8 * t + 6, "sw", send_w.at[t, bottom], east.at[t, before]),
            (8 * t + 7, "nw", send_w.at[t, top], east.at[t, after]),
        )

    for t in range(STEPS):
        load_e[t].wait()
        for target, first, turn in ((send_e, tile - reach, 0), (send_w, 0, 2)):
            packed = None
            for s in range(species):
                place = (s + turn) % species
                moved = pltpu.roll(e_v[t, s], (reach * place - first) % tile, 1)
                packed = moved if packed is None else jnp.where(slot == place, moved, packed)
            target[t] = packed
        if t == 0:
            peers = sum(has[side].astype(jnp.int32) for side in has)
            pl.semaphore_wait(barrier, peers)
        for args in strip_args(t) + corner_args(t) + row_args(t):
            send(*args)

    kpad[...] = jnp.zeros(kpad.shape, F32)
    width = 2 * reach + 1
    for copy in load_k:
        copy.wait()
    for s in range(species):
        kpad[s, :width, :width] = k_v[:, s, :]
    def even_odd(value):
        u, w = value[:tile, :tile], value[:tile, tile:]
        z, v = value[tile:, :tile], value[tile:, tile:]
        return u + v, w - z, u - v, w + z

    for s in range(species):
        first = dot3(split(kpad[s]), (v_ck[0], v_ck[1]))
        second = dot3((v_kr[0], v_kr[1]), split(first))
        for position, value in enumerate(even_odd(second)):
            kspec[s, position] = value

    def own_part(t):
        for s in range(species):
            high, low = split(e_v[t, s])
            xh[s, :tile, :tile] = high
            xl[s, :tile, :tile] = low

    def rows_part(t):
        for s in range(species):
            high, low = split(ns[t, s])
            xh[s, tile:, :tile] = high
            xl[s, tile:, :tile] = low

    def cols_part(t):
        wide = lax.broadcasted_iota(jnp.int32, (tile + 2 * reach, tile), 1)
        from_west, from_east = west[t], east[t]
        left = wide < tile // 2
        for pair in range(2):
            joined = jnp.where(left, from_west, from_east) if pair == 0 else jnp.where(left, from_east, from_west)
            for odd in range(2):
                s = 2 * pair + odd
                mine = jnp.where((wide // reach) % 2 == odd, joined, 0.0)
                high, low = split(mine)
                xh[s, :, tile:] = high
                xl[s, :, tile:] = low

    def disperse(t):
        span = tile + 2 * reach
        firsts = []
        for pair, table in enumerate((v_ca, v_cb)):
            both = pl.ds(2 * pair, 2)
            x = tuple(ref[both].reshape(2 * span, 2 * tile) for ref in (xh, xl))
            a = dot3(x, (table[0], table[1]))
            firsts += [split(a[:span]), split(a[span:])]
        seconds = [dot3((v_rf[0], v_rf[1]), a) for a in firsts]
        spectra = []
        for s in range(species):
            pr, pi, mr, mi = even_odd(seconds[s])
            kpr, kpi, kmr, kmi = (kspec[s, n] for n in range(4))
            gpr = pr * kpr - pi * kpi
            gpi = pr * kpi + pi * kpr
            gmr = mr * kmr - mi * kmi
            gmi = mr * kmi + mi * kmr
            top = jnp.concatenate([gpr + gmr, gpi + gmi], axis=1)
            bottom = jnp.concatenate([gmi - gpi, gpr - gmr], axis=1)
            spectra.append(split(jnp.concatenate([top, bottom], axis=0)))
        thirds = [split(dot3((v_ri[0], v_ri[1]), g)) for g in spectra]
        for s in range(species):
            src[t, s] = dot3(thirds[s], (v_ci[0], v_ci[1]))

    first_row = 8
    inner = pl.ds(first_row, tile)
    packed_rows = c_send.shape[1]

    def edge_args(t):
        base = 16 + 4 * t
        return (
            (base + 0, "n", n_send.at[t], s_recv.at[t]),
            (base + 1, "s", s_send.at[t], n_recv.at[t]),
            (base + 2, "w", c_send.at[t], e_recv.at[t]),
            (base + 3, "e", c_send.at[t], w_recv.at[t]),
        )

    def mix_and_send(t, state):
        packed = jnp.zeros((tile, tile), F32)
        for s in range(species):
            for k in range(boxes):
                f = s * boxes + k
                m = decay[s, k] * state[s, k] + fraction[s, k] * src[t, s]
                mix[f, inner, :] = m
                n_send[t, f : f + 1, :] = m[0:1, :]
                s_send[t, f : f + 1, :] = m[tile - 1 : tile, :]
                packed = jnp.where(lane // 2 == f, pltpu.roll(m, 2 * f + 1, 1), packed)
        c_send[t] = packed.T[:packed_rows]
        for args in edge_args(t):
            send(*args)

    def coefficients(t):
        u, v = w_v[t, 0], w_v[t, 1]
        up, um = jnp.maximum(u, 0.0), jnp.minimum(u, 0.0)
        vp, vm = jnp.maximum(v, 0.0), jnp.minimum(v, 0.0)
        coef[0] = (1.0 - 4.0 * DIFFUSION) - up + um - vp + vm
        to_west, to_east = up + DIFFUSION, DIFFUSION - um
        coef[1] = jnp.where(lane > 0, to_west, 0.0)
        coef[2] = jnp.where(lane < tile - 1, to_east, 0.0)
        coef[3] = vp + DIFFUSION
        coef[4] = DIFFUSION - vm
        coef[5] = jnp.where(lane == 0, to_west, jnp.where(lane == tile - 1, to_east, 0.0))

    def stencil(f):
        m = mix[f, inner, :]
        return (
            coef[0] * m
            + coef[1] * pltpu.roll(m, 1, 1)
            + coef[2] * pltpu.roll(m, tile - 1, 1)
            + coef[3] * mix[f, pl.ds(first_row - 1, tile), :]
            + coef[4] * mix[f, pl.ds(first_row + 1, tile), :]
        )

    def beside(t):
        odd = lax.broadcasted_iota(jnp.int32, (packed_rows, tile), 0) % 2 == 1
        joined = jnp.where(
            odd, pltpu.roll(w_recv[t], 1, 0), pltpu.roll(e_recv[t], packed_rows - 1, 0)
        )
        return jnp.concatenate([joined, jnp.zeros((tile - packed_rows, tile), F32)], axis=0).T

    def from_sides(halo, f):
        return coef[5] * pltpu.roll(halo, (tile - 2 * f - 1) % tile, 1)

    def transport_first(t, result):
        for args in edge_args(t):
            wait_recv(*args)
        for f in range(species * boxes):
            mix[f, first_row - 1 : first_row, :] = n_recv[t, f : f + 1, :]
            mix[f, first_row + tile : first_row + tile + 1, :] = s_recv[t, f : f + 1, :]
        halo = beside(t)
        for f in range(species * boxes):
            result[f // boxes, f % boxes] = stencil(f) + from_sides(halo, f)

    def transport_last(t):
        north, south = coef[3, 0:1, :], coef[4, tile - 1 : tile, :]
        coef[3] = jnp.where(row > 0, coef[3], 0.0)
        coef[4] = jnp.where(row < tile - 1, coef[4], 0.0)
        side_coef[...] = coef[5]
        for s in range(species):
            for k in range(boxes):
                o_v[s, k] = stencil(s * boxes + k)
            pltpu.make_async_copy(o_v.at[s], part.at[s], osem.at[s]).start()
        for args in edge_args(t):
            wait_recv(*args)
        side_halo[...] = beside(t)
        for s in range(species):
            fields = slice(s * boxes, (s + 1) * boxes)
            row_halo[0, s] = north * n_recv[t, fields, :]
            row_halo[1, s] = south * s_recv[t, fields, :]

    def source(t):
        own_part(t)
        for args in row_args(t):
            wait_recv(*args)
        rows_part(t)
        for args in strip_args(t) + corner_args(t):
            wait_recv(*args)
        cols_part(t)
        disperse(t)

    for copy in load_t:
        copy.wait()
    source(0)
    load_s.wait()
    load_w.wait()
    mix_and_send(0, s_v)
    source(1)
    coefficients(0)
    transport_first(0, s_v)
    mix_and_send(1, s_v)
    coefficients(1)
    transport_last(1)
    for channel, side, sent, target in sends:
        @pl.when(has[side])
        def _():
            remote(channel, side, sent, target).wait_send()
    for s in range(species):
        pltpu.make_async_copy(o_v.at[s], part.at[s], osem.at[s]).wait()


def finish(tile, part, side_halo, side_coef, row_halo, out, surf, p_v, h_v, c_v, r_v, f_v, isem, osem):
    species, boxes = part.shape[:2]
    pairs = [(side_halo, h_v), (side_coef, c_v), (row_halo, r_v)]
    pairs += [(part.at[s], p_v.at[s]) for s in range(species)]
    loads = [pltpu.make_async_copy(a, b, isem.at[n]) for n, (a, b) in enumerate(pairs)]
    for copy in loads:
        copy.start()
    for copy in loads[:3]:
        copy.wait()
    stores = []
    for s in range(species):
        loads[3 + s].wait()
        summed = None
        for k in range(boxes):
            turn = (tile - 2 * (s * boxes + k) - 1) % tile
            value = p_v[s, k] + c_v[...] * pltpu.roll(h_v[...], turn, 1)
            p_v[s, k] = value
            p_v[s, k, 0:1] += r_v[0, s, k : k + 1]
            p_v[s, k, tile - 1 :] += r_v[1, s, k : k + 1]
            summed = value if summed is None else summed + value
        f_v[s] = summed
        f_v[s, 0:1] += jnp.sum(r_v[0, s], axis=0, keepdims=True)
        f_v[s, tile - 1 :] += jnp.sum(r_v[1, s], axis=0, keepdims=True)
        stores.append(pltpu.make_async_copy(p_v.at[s], out.at[s], osem.at[2 * s]))
        stores.append(pltpu.make_async_copy(f_v.at[s], surf.at[s], osem.at[2 * s + 1]))
        for copy in stores[-2:]:
            copy.start()
    for copy in stores:
        copy.wait()


def on_device(rows, cols, emissions, winds, kernels, box_states, decay, fraction):
    _, species, tile, _ = emissions.shape
    boxes = box_states.shape[1]
    reach = (kernels.shape[-1] - 1) // 2
    fields = species * boxes
    tabs = [jnp.asarray(t) for t in tables(tile, reach, tile)]
    hbm = pl.BlockSpec(memory_space=pltpu.HBM)
    vmem = pl.BlockSpec(memory_space=pltpu.VMEM)
    smem = pl.BlockSpec(memory_space=pltpu.SMEM)
    span = tile + 2 * reach

    def buf(*shape, dtype=F32):
        return pltpu.VMEM(shape, dtype)

    channels = 16 + 4 * STEPS
    partial = tuple(
        pl.pallas_call(
            functools.partial(kernel, rows, cols, tile, reach),
            out_shape=(
                jax.ShapeDtypeStruct(box_states.shape, F32),
                jax.ShapeDtypeStruct((tile, tile), F32),
                jax.ShapeDtypeStruct((tile, tile), F32),
                jax.ShapeDtypeStruct((2, species, boxes, tile), F32),
            ),
            in_specs=[hbm, hbm, hbm, hbm, smem, smem] + [hbm] * len(tabs),
            out_specs=(hbm, vmem, vmem, vmem),
            scratch_shapes=[
                buf(STEPS, species, tile, tile),
                buf(STEPS, 2, tile, tile),
                buf(species, boxes, tile, tile),
                buf(species, boxes, tile, tile),
                buf(2 * reach + 1, species, 2 * reach + 1),
            ]
            + [buf(*t.shape, dtype=BF16) for t in tabs]
            + [
                buf(species, tile, tile),
                buf(species, 4, tile, tile),
                buf(STEPS, tile, tile),
                buf(STEPS, tile, tile),
                buf(STEPS, span, tile),
                buf(STEPS, span, tile),
                buf(STEPS, species, 2 * reach, tile),
                buf(species, span, 2 * tile, dtype=BF16),
                buf(species, span, 2 * tile, dtype=BF16),
                buf(fields, tile + 16, tile),
                buf(STEPS, species, tile, tile),
                buf(STEPS, fields, tile),
                buf(STEPS, fields, tile),
                buf(STEPS, fields, tile),
                buf(STEPS, fields, tile),
                buf(STEPS, 2 * fields, tile),
                buf(STEPS, 2 * fields, tile),
                buf(STEPS, 2 * fields, tile),
                buf(6, tile, tile),
                pltpu.SemaphoreType.DMA((STEPS + len(tabs) + 3,)),
                pltpu.SemaphoreType.DMA((channels,)),
                pltpu.SemaphoreType.DMA((channels,)),
                pltpu.SemaphoreType.DMA((species,)),
            ],
            compiler_params=pltpu.CompilerParams(
                collective_id=0, has_side_effects=True, vmem_limit_bytes=61 * 2**20
            ),
        )(emissions, winds, kernels.transpose(1, 0, 2), box_states, decay, fraction, *tabs)
    )
    return tuple(
        pl.pallas_call(
            functools.partial(finish, tile),
            out_shape=(
                jax.ShapeDtypeStruct(box_states.shape, F32),
                jax.ShapeDtypeStruct((species, tile, tile), F32),
            ),
            in_specs=[hbm] * 4,
            out_specs=(hbm, hbm),
            scratch_shapes=[
                buf(species, boxes, tile, tile),
                buf(tile, tile),
                buf(tile, tile),
                buf(2, species, boxes, tile),
                buf(species, tile, tile),
                pltpu.SemaphoreType.DMA((3 + species,)),
                pltpu.SemaphoreType.DMA((2 * species,)),
            ],
            compiler_params=pltpu.CompilerParams(vmem_limit_bytes=61 * 2**20),
        )(*partial)
    )


def solution(mesh):
    placed = (
        P(None, None, "row", "col"),
        P(None, None, "row", "col"),
        P(),
        P(None, None, "row", "col"),
        P(),
        P(),
    )
    return jax.shard_map(
        functools.partial(on_device, mesh.shape["row"], mesh.shape["col"]),
        mesh=mesh,
        in_specs=placed,
        out_specs=(P(None, None, "row", "col"), P(None, "row", "col")),
        check_vma=False,
    )
```
